256 devices in a mesh: rx: 32 (over z, x_hi, core), tm: 8 (over y, x_lo).
Axes of the slice: x: 4 (x_hi: 2, x_lo: 2; x = x_hi * 2 + x_lo), y: 4, z: 8, core: 2. Of those that a mesh axis runs over, the one named last changes fastest.
Arguments:
- records: float32 [4096, 24576], P('rx', 'tm'), may hold values from -1000 to 1000, as said below
- source_block: int32 [2], replicated, may hold values from 0 to 63
- quality: int32 [4096], P('rx'), may hold values 0 or 1
Outputs:
- stacks: float32 [2, 64, 101, 4096], P(None, 'tm', None, 'rx')
The draws below stay inside these ranges and needn't reach their ends.
Inputs may be any that keep to these rules, and one draw needn't show every extreme that they name: Noise records with channel and window gains.
All inputs are finite; a program needn't handle non-finite values. No bound on the sum of `quality` on one device may be relied on, other than what follows from the above.
Results may differ from the reference program's by a relative error of at most 0.0039.
Values may be sent and summed in bfloat16 or wider, within the bound.
A program may use at most 192 MiB of HBM per device.

```python
import math
import jax
import jax.numpy as jnp
from jax import lax

W = 1024
HALF = 50
LAGS = 101
SRC = 64
STEPS = 2
CHANNELS = 4096
WINDOWS = 24
BLOCKS = 64


def draw_records(key, part):
    key_noise, key_channel, key_window = jax.random.split(key, 3)
    shape_full = (CHANNELS, WINDOWS, W)
    channel_gain = jnp.exp(jax.random.uniform(key_channel, (CHANNELS, 1, 1)) * math.log(10.0))
    window_gain = jnp.exp(jax.random.uniform(key_window, (CHANNELS, WINDOWS, 1)) * math.log(10.0))
    noise = jnp.clip(jax.random.normal(key_noise, shape_full), -8.0, 8.0)
    scaled = noise * channel_gain * window_gain
    return scaled.reshape(CHANNELS, WINDOWS * W).astype(jnp.float32)


def with_ends(values, key, least, top_value):
    extent = values.shape
    index_at = [jax.random.randint(jax.random.fold_in(key, axis), (), 0, extent[axis]) for axis in range(len(extent))]
    values = values.at[tuple(index_at)].set(least)
    longest = extent.index(max(extent))
    index_at[longest] = (index_at[longest] + 1) % extent[longest]
    return values.at[tuple(index_at)].set(top_value)


def setup_inputs(seed: int = 0) -> dict:
    key_of = jax.random.split(jax.random.key(seed), 4)
    return {
        "records": draw_records(jax.random.fold_in(key_of[3], 71), 0),
        "source_block": jax.random.randint(key_of[1], (STEPS,), 0, BLOCKS).astype(jnp.int32),
        "quality": with_ends((jax.random.randint(key_of[2], (CHANNELS,), 0, 8) < 7).astype(jnp.int32), jax.random.fold_in(key_of[2], 1), 0, 1),
    }


def reference(records, source_block, quality):
    samples = records.reshape(CHANNELS, WINDOWS, W)
    power = lax.optimization_barrier(jnp.mean(samples * samples, axis=2, keepdims=True))
    whitened = (samples * lax.rsqrt(power + 1e-06) * quality.astype(jnp.float32)[:, None, None]).astype(jnp.bfloat16)
    widened = whitened.astype(jnp.float32)
    padded = jnp.pad(widened, ((0, 0), (0, 0), (HALF, HALF)))
    weight = 1.0 / math.sqrt(W * WINDOWS)
    results = []
    for number in range(STEPS):
        first_row = (source_block[number] * SRC).astype(jnp.int32)
        sources = lax.dynamic_slice_in_dim(widened, first_row, SRC, 0)

        def one_lag(lag_index):
            shifted = lax.dynamic_slice_in_dim(padded, lag_index, W, 2)
            return jnp.einsum('snt,rnt->sr', sources, shifted, precision=lax.Precision.HIGHEST)
        lagged = lax.map(one_lag, jnp.arange(LAGS, dtype=jnp.int32))
        results.append(jnp.transpose(lagged, (1, 0, 2)) * weight)
    return jnp.stack(results, 0)
```

```python
import math

import jax
import jax.numpy as jnp
from jax import lax
from jax.experimental import pallas as pl
from jax.experimental.pallas import tpu as pltpu
from jax.sharding import PartitionSpec as P

W = 1024
LAGS = 101
FINE = 8
COARSE = 13
PAD = 48
NZ = 8
NY = 4
WIN = 3
ROWS = W + 2 * PAD
SHARE = WIN * W
PIECE = SHARE // NZ
PAIRS = (COARSE + 1) // 2
WEIGHT = 1.0 / math.sqrt(24 * W)
MESH = pl.DeviceIdType.MESH
F32 = jnp.float32
BF16 = jnp.bfloat16


def device(z, xh, c, y, xl):
    return ((z * 2 + xh) * 2 + c, y * 2 + xl)


def shifted_rows(values, shift):
    return pltpu.roll(values, shift % values.shape[1], 1)


def fill_second_lane_half(ab, w, columns):
    zeros = jnp.zeros((8, 128), F32)
    ab[w, PAD - 16 : PAD + W, 128:256] = jnp.concatenate([zeros, columns, zeros], 0).astype(BF16)


def edge_rows(block, keep_low):
    blocks = block.reshape(PAD // 8, 8, 128)
    rolled = pltpu.roll(blocks, 2, 1)
    row = lax.broadcasted_iota(jnp.int32, rolled.shape, 1)
    keep = row < 2 if keep_low else row >= 2
    return jnp.where(keep, rolled, 0.0)


def fill_edges(re32, w, head, tail):
    low = edge_rows(head, True)
    high = edge_rows(tail, False)
    at = pl.ds(pl.multiple_of(w * 8, 8), 8)
    for m in range(1, PAD // 8 + 1):
        c = 6 + m
        re32[c // 2, at, (c % 2) * 128 : (c % 2) * 128 + 128] = low[m - 1]
        c = 6 - m
        re32[c // 2, at, (c % 2) * 128 : (c % 2) * 128 + 128] = high[PAD // 8 - m]


def kernel(
    rec, blk, qual, out,
    wh, v, mrg, rsb, piece, s, ab, re32, re, lhs, lext, own, snd, rcv,
    mrg_s, mrg_r, rs_s, rs_r, ag_s, ag_r, x_s, x_r, cx_s, cx_r, y_s, y_r,
):
    rx = lax.axis_index("rx")
    tm = lax.axis_index("tm")
    z, xh, c = rx // 4, (rx // 2) % 2, rx % 2
    y, xl = tm // 2, tm % 2

    def plane_peer(i):
        return (z + i // 4) % NZ, (xh + (i // 2) % 2) % 2, (xl + i % 2) % 2

    barrier = pltpu.get_barrier_semaphore()

    def greet(i, _):
        pz, pxh, pxl = plane_peer(i)
        pl.semaphore_signal(barrier, inc=1, device_id=device(pz, pxh, c, y, pxl), device_id_type=MESH)
        return 0

    lax.fori_loop(1, 4 * NZ, greet, 0)
    pl.semaphore_signal(barrier, inc=1, device_id=device(z, xh, 1 - c, y, xl), device_id_type=MESH)
    for g in range(1, NY):
        pl.semaphore_signal(barrier, inc=1, device_id=device(z, xh, c, (y + g) % NY, xl), device_id_type=MESH)

    ones = jnp.broadcast_to(qual[...].astype(F32), (128, 128))
    usable = jnp.transpose(ones)[:, :1]
    marks = []
    for k in range(2):
        b = blk[k]
        for half in range(2):
            marks.append((b == rx * 2 + half).astype(F32))
    for w in range(WIN):
        x = rec[:, w * W : (w + 1) * W]
        power = jnp.sum(x * x, axis=1, keepdims=True) * (1.0 / W)
        white = x * (lax.rsqrt(power + 1e-06) * usable)
        wh[:, w * W : (w + 1) * W] = white
        for t in range(2 * NY):
            rows = [
                white[8 * t : 8 * t + 8] * marks[2 * k] + white[64 + 8 * t : 72 + 8 * t] * marks[2 * k + 1]
                for k in range(2)
            ]
            v[t % 2, t // 2, :, w * W : (w + 1) * W] = jnp.concatenate(rows, 0).astype(BF16)

    pl.semaphore_wait(barrier, 4 * NZ - 1 + 1 + NY - 1)

    merge = pltpu.make_async_remote_copy(
        src_ref=v.at[:, pl.ds(2 * (1 - c), 2)], dst_ref=mrg, send_sem=mrg_s, recv_sem=mrg_r,
        device_id=device(z, xh, 1 - c, y, xl), device_id_type=MESH,
    )
    merge.start()

    def exchange(w):
        slot = ab.at[xl * WIN + w, pl.ds(PAD, W), pl.ds(0, 128)]
        return pltpu.make_async_remote_copy(
            src_ref=slot, dst_ref=slot, send_sem=x_s.at[w], recv_sem=x_r.at[w],
            device_id=device(z, xh, c, y, 1 - xl), device_id_type=MESH,
        )

    def scatter(i):
        pz, pxh = (z + i // 2) % NZ, (xh + i % 2) % 2
        return pltpu.make_async_remote_copy(
            src_ref=v.at[:, 2 * c + pxh, :, pl.ds(pl.multiple_of(pz * PIECE, 128), PIECE)],
            dst_ref=rsb.at[i], send_sem=rs_s.at[i], recv_sem=rs_r.at[i],
            device_id=device(pz, pxh, c, y, xl), device_id_type=MESH,
        )

    my_lanes = pl.ds(pl.multiple_of(xl * SHARE + z * PIECE, 128), PIECE)

    def gather(i):
        pz, pxh, pxl = plane_peer(i)
        return pltpu.make_async_remote_copy(
            src_ref=piece.at[pxl], dst_ref=s.at[2 * c + xh, :, my_lanes],
            send_sem=ag_s.at[i], recv_sem=ag_r.at[i],
            device_id=device(pz, pxh, c, y, pxl), device_id_type=MESH,
        )

    merge.wait()
    v[:, pl.ds(2 * c, 2)] = v[:, pl.ds(2 * c, 2)] + mrg[...]

    def run(fn):
        def step(i, _):
            fn(i)
            return 0
        return step

    lax.fori_loop(1, 2 * NZ, run(lambda i: scatter(i).start()), 0)

    zero_rows = jnp.zeros((PAD, 256), BF16)
    for w in range(2 * WIN):
        ab[w, 0:PAD, :] = zero_rows
        ab[w, PAD + W : ROWS, :] = zero_rows
    re32[...] = jnp.zeros_like(re32)
    for w in range(WIN):
        columns = jnp.transpose(wh[:, w * W : (w + 1) * W])
        at = xl * WIN + w
        ab[at, PAD : PAD + W, 0:128] = columns.astype(BF16)
        exchange(w).start()
        columns = columns.astype(BF16).astype(F32)
        fill_second_lane_half(ab, at, columns)
        fill_edges(re32, at, columns[:PAD], columns[W - PAD :])

    lax.fori_loop(1, 2 * NZ, run(lambda i: scatter(i).wait()), 0)
    total = v[:, 2 * c + xh, :, pl.ds(pl.multiple_of(z * PIECE, 128), PIECE)]
    total = lax.fori_loop(1, 2 * NZ, lambda i, t: t + rsb[i], total)
    piece[...] = total
    lax.fori_loop(1, 4 * NZ, run(lambda i: gather(i).start()), 0)
    s[2 * c + xh, :, my_lanes] = piece[xl]

    for w in range(WIN):
        at = (1 - xl) * WIN + w
        exchange(w).wait()
        columns = ab[at, PAD : PAD + W, 0:128].astype(F32)
        fill_second_lane_half(ab, at, columns)
        fill_edges(re32, at, columns[:PAD], columns[W - PAD :])
    re[...] = re32[...].astype(BF16)

    lax.fori_loop(1, 4 * NZ, run(lambda i: gather(i).wait()), 0)
    halves = s.at[pl.ds(2 * c, 2)]
    swap = pltpu.make_async_remote_copy(
        src_ref=halves, dst_ref=halves, send_sem=cx_s, recv_sem=cx_r,
        device_id=device(z, xh, 1 - c, y, xl), device_id_type=MESH,
    )
    swap.start()

    lane = lax.broadcasted_iota(jnp.int32, (16, 128), 1)

    def expand(group):
        top = pl.multiple_of(((group + NY - y) % NY) * 128, 128)

        def window(w, ext):
            x = s[group, :, pl.ds(pl.multiple_of(w * W, W), W)].astype(F32)
            results = []
            for f in range(FINE):
                shift = f - 2
                rows = pl.ds(pl.multiple_of(top + f * 16, 16), 16)
                moved = shifted_rows(x, shift)
                if shift > 0:
                    wraps, tile = lane < shift, 0
                else:
                    wraps, tile = lane >= 128 + shift, W - 128
                edge = moved[:, tile : tile + 128]
                kept = jnp.where(wraps, 0.0, edge)
                if tile == 0:
                    moved = jnp.concatenate([kept, moved[:, 128:]], 1)
                else:
                    moved = jnp.concatenate([moved[:, :tile], kept], 1)
                lhs[rows, pl.ds(pl.multiple_of(w * W, W), W)] = moved.astype(BF16)
                lost = jnp.where(wraps, edge, 0.0)
                results.append(ext[f] + pltpu.roll(lost, w * 8 + 2, 1))
            return tuple(results)

        ext = lax.fori_loop(0, 2 * WIN, window, tuple(jnp.zeros((16, 128), F32) for _ in range(FINE)))
        for f in range(FINE):
            rows = pl.ds(pl.multiple_of(top + f * 16, 16), 16)
            lext[rows, :] = ext[f].astype(BF16)

    lax.fori_loop(0, 2, run(lambda j: expand(2 * c + j)), 0)
    swap.wait()
    lax.fori_loop(0, 2, run(lambda j: expand(2 * (1 - c) + j)), 0)

    def reduce_copy(g, p, lanes=256):
        return pltpu.make_async_remote_copy(
            src_ref=snd.at[g - 1, p, :, pl.ds(0, lanes)], dst_ref=rcv.at[g - 1, p, :, pl.ds(0, lanes)],
            send_sem=y_s.at[g - 1, p], recv_sem=y_r.at[g - 1, p],
            device_id=device(z, xh, c, (y + g) % NY, xl), device_id_type=MESH,
        )

    def correlate(p, lanes=256):
        acc = jnp.dot(lext[...], re[p, :, :lanes], preferred_element_type=F32)
        for w in range(2 * WIN):
            acc += jnp.dot(
                lhs[:, w * W : (w + 1) * W],
                ab[w, pl.ds(pl.multiple_of(p * 16, 16), W), 0:lanes],
                preferred_element_type=F32,
            )
        own[p, :, :lanes] = acc[:128]
        for g in range(1, NY):
            snd[g - 1, p, :, :lanes] = acc[128 * g : 128 * g + 128].astype(BF16)
            reduce_copy(g, p, lanes).start()

    lax.fori_loop(0, PAIRS - 1, run(correlate), 0)
    correlate(PAIRS - 1, 128)

    def finish(p, lanes=256):
        for g in range(1, NY):
            reduce_copy(g, p, lanes).wait()
        acc = own[p, :, :lanes]
        for g in range(1, NY):
            acc += rcv[g - 1, p, :, :lanes].astype(F32)
        acc *= WEIGHT
        for h in range(lanes // 128):
            out[2 * p + h] = acc[:, 128 * h : 128 * h + 128]

    lax.fori_loop(0, PAIRS - 1, run(finish), 0)
    finish(PAIRS - 1, 128)


def on_device(records, source_block, quality):
    vmem = pl.BlockSpec(memory_space=pltpu.VMEM)
    dma = pltpu.SemaphoreType.DMA
    sums = pl.pallas_call(
        kernel,
        out_shape=jax.ShapeDtypeStruct((COARSE, 128, 128), F32),
        in_specs=[vmem, pl.BlockSpec(memory_space=pltpu.SMEM), vmem],
        out_specs=vmem,
        scratch_shapes=[
            pltpu.VMEM((128, SHARE), F32),
            pltpu.VMEM((2, NY, 16, SHARE), BF16),
            pltpu.VMEM((2, 2, 16, SHARE), BF16),
            pltpu.VMEM((2 * NZ, 2, 16, PIECE), BF16),
            pltpu.VMEM((2, 16, PIECE), BF16),
            pltpu.VMEM((NY, 16, 2 * SHARE), BF16),
            pltpu.VMEM((2 * WIN, ROWS, 256), BF16),
            pltpu.VMEM((PAIRS, 128, 256), F32),
            pltpu.VMEM((PAIRS, 128, 256), BF16),
            pltpu.VMEM((NY * 128, 2 * SHARE), BF16),
            pltpu.VMEM((NY * 128, 128), BF16),
            pltpu.VMEM((PAIRS, 128, 256), F32),
            pltpu.VMEM((NY - 1, PAIRS, 128, 256), BF16),
            pltpu.VMEM((NY - 1, PAIRS, 128, 256), BF16),
            dma, dma, dma((2 * NZ,)), dma((2 * NZ,)), dma((4 * NZ,)), dma((4 * NZ,)),
            dma((WIN,)), dma((WIN,)), dma, dma, dma((NY - 1, PAIRS)), dma((NY - 1, PAIRS)),
        ],
        compiler_params=pltpu.CompilerParams(
            collective_id=0, has_side_effects=True, vmem_limit_bytes=56 << 20
        ),
        name="correlate",
    )(records, source_block, quality.reshape(1, 128))
    stacks = sums.reshape(COARSE, FINE, 2, 8, 128).transpose(2, 3, 0, 1, 4)
    return stacks.reshape(2, 8, COARSE * FINE, 128)[:, :, :LAGS]


def solution(mesh):
    in_specs = (P("rx", "tm"), P(), P("rx"))
    out_specs = P(None, "tm", None, "rx")
    return jax.shard_map(
        on_device, mesh=mesh, in_specs=in_specs, out_specs=out_specs, check_vma=False
    )
```

```python
import math

import jax
import jax.numpy as jnp
from jax import lax
from jax.experimental import pallas as pl
from jax.experimental.pallas import tpu as pltpu
from jax.sharding import PartitionSpec as P

W = 1024
LAGS = 101
FINE = 8
COARSE = 13
PAD = 48
NZ = 8
NY = 4
WIN = 3
ROWS = W + 2 * PAD
SHARE = WIN * W
PIECE = SHARE // NZ
PAIRS = (COARSE + 1) // 2
WEIGHT = 1.0 / math.sqrt(24 * W)
MESH = pl.DeviceIdType.MESH
F32 = jnp.float32
BF16 = jnp.bfloat16


def device(z, xh, c, y, xl):
    return ((z * 2 + xh) * 2 + c, y * 2 + xl)


def shifted_rows(values, shift):
    return pltpu.roll(values, shift % values.shape[1], 1)


def fill_second_lane_half(ab, w, columns):
    zeros = jnp.zeros((8, 128), F32)
    ab[w, PAD - 16 : PAD + W, 128:256] = jnp.concatenate([zeros, columns, zeros], 0).astype(BF16)


def edge_rows(block, keep_low):
    blocks = block.reshape(PAD // 8, 8, 128)
    rolled = pltpu.roll(blocks, 2, 1)
    row = lax.broadcasted_iota(jnp.int32, rolled.shape, 1)
    keep = row < 2 if keep_low else row >= 2
    return jnp.where(keep, rolled, 0.0)


def fill_edges(re32, w, head, tail):
    low = edge_rows(head, True)
    high = edge_rows(tail, False)
    at = pl.ds(pl.multiple_of(w * 8, 8), 8)
    for m in range(1, PAD // 8 + 1):
        c = 6 + m
        re32[c // 2, at, (c % 2) * 128 : (c % 2) * 128 + 128] = low[m - 1]
        c = 6 - m
        re32[c // 2, at, (c % 2) * 128 : (c % 2) * 128 + 128] = high[PAD // 8 - m]


def kernel(
    rec, blk, qual, out,
    wh, v, mrg, rsb, piece, s, ab, re32, re, lhs, lext, own, ysnd, yrcv, xsnd, xrcv,
    mrg_s, mrg_r, rs_s, rs_r, ag_s, ag_r, ex_s, ex_r, cx_s, cx_r, y_s, y_r, x_s, x_r, ready,
):
    rx = lax.axis_index("rx")
    tm = lax.axis_index("tm")
    z, xh, c = rx // 4, (rx // 2) % 2, rx % 2
    y, xl = tm // 2, tm % 2
    sibling = device(z, xh, 1 - c, y, xl)

    def plane_peer(i):
        return (z + i // 2) % NZ, (xh + i % 2) % 2

    def run(fn):
        def step(i, _):
            fn(i)
            return 0

        return step

    barrier = pltpu.get_barrier_semaphore()

    def greet(peer):
        pl.semaphore_signal(barrier, inc=1, device_id=peer, device_id_type=MESH)

    greet(sibling)
    lax.fori_loop(1, 2 * NZ, run(lambda i: greet(device(*plane_peer(i), c, y, xl))), 0)
    for g in range(1, NY):
        greet(device(z, xh, c, (y + g) % NY, xl))
    greet(device(z, xh, c, y, 1 - xl))

    ones = jnp.broadcast_to(qual[...].astype(F32), (128, 128))
    usable = jnp.transpose(ones)[:, :1]
    marks = []
    for k in range(2):
        b = blk[k]
        for half in range(2):
            marks.append((b == rx * 2 + half).astype(F32))
    for w in range(WIN):
        x = rec[:, w * W : (w + 1) * W]
        power = jnp.sum(x * x, axis=1, keepdims=True) * (1.0 / W)
        white = x * (lax.rsqrt(power + 1e-06) * usable)
        wh[:, w * W : (w + 1) * W] = white
        for k in range(2):
            rows = white[:64] * marks[2 * k] + white[64:] * marks[2 * k + 1]
            v[k, :, :, w * W : (w + 1) * W] = rows.astype(BF16).reshape(NY, 16, W)

    zero_rows = jnp.zeros((PAD, 256), BF16)
    for w in range(2 * WIN):
        ab[w, 0:PAD, :] = zero_rows
        ab[w, PAD + W : ROWS, :] = zero_rows
    re32[...] = jnp.zeros_like(re32)
    for w in range(WIN):
        columns = jnp.transpose(wh[:, w * W : (w + 1) * W]).astype(BF16)
        at = (y // 2) * WIN + w
        ab[at, PAD : PAD + W, 0:128] = columns
        columns = columns.astype(F32)
        fill_second_lane_half(ab, at, columns)
        fill_edges(re32, at, columns[:PAD], columns[W - PAD :])

    pl.semaphore_wait(barrier, 1 + (2 * NZ - 1) + NY)
    pl.semaphore_signal(ready, inc=1, device_id=device(z, xh, c, (y + 2) % NY, xl), device_id_type=MESH)

    def merge(j):
        yd = (y + 1 + 2 * j + j // 2) % NY
        return pltpu.make_async_remote_copy(
            src_ref=v.at[1 - c, yd], dst_ref=mrg.at[yd], send_sem=mrg_s.at[j], recv_sem=mrg_r.at[j],
            device_id=sibling, device_id_type=MESH,
        )

    def exchange(w):
        slot = ab.at[(y // 2) * WIN + w, pl.ds(PAD, W), pl.ds(0, 128)]
        return pltpu.make_async_remote_copy(
            src_ref=slot, dst_ref=slot, send_sem=ex_s.at[w], recv_sem=ex_r.at[w],
            device_id=device(z, xh, c, (y + 2) % NY, xl), device_id_type=MESH,
        )

    def group_of(h, xd):
        if h == 0:
            return (y + 3 + 2 * ((c + xd) % 2)) % NY
        return (y + 2 * xd) % NY

    def scatter(h, i):
        pz, pxh = plane_peer(i)
        return pltpu.make_async_remote_copy(
            src_ref=v.at[c, group_of(h, pxh), :, pl.ds(pl.multiple_of(pz * PIECE, 128), PIECE)],
            dst_ref=rsb.at[h, i], send_sem=rs_s.at[h, i], recv_sem=rs_r.at[h, i],
            device_id=device(pz, pxh, c, y, xl), device_id_type=MESH,
        )

    my_lanes = pl.ds(pl.multiple_of((y // 2) * SHARE + z * PIECE, 128), PIECE)

    def gather(h, i):
        return pltpu.make_async_remote_copy(
            src_ref=piece.at[h], dst_ref=s.at[h, c, :, my_lanes],
            send_sem=ag_s.at[h, i], recv_sem=ag_r.at[h, i],
            device_id=device(*plane_peer(i), c, (y + 2 * xh) % NY, xl), device_id_type=MESH,
        )

    def swap(h):
        return pltpu.make_async_remote_copy(
            src_ref=s.at[h, c], dst_ref=s.at[h, c], send_sem=cx_s.at[h], recv_sem=cx_r.at[h],
            device_id=sibling, device_id_type=MESH,
        )

    for j in range(NY):
        merge(j).start()
    for w in range(WIN):
        exchange(w).start()
    def scatter_half(h):
        for j in range(2):
            merge(2 * h + j).wait_recv()
            yd = (y + 1 + 2 * j + h) % NY
            v[c, yd] = v[c, yd] + mrg[yd]
        for i in range(1, 2 * NZ):
            scatter(h, i).start()

    def gather_half(h):
        total = v[c, group_of(h, xh), :, pl.ds(pl.multiple_of(z * PIECE, 128), PIECE)]
        for i in range(1, 2 * NZ):
            scatter(h, i).wait_recv()
            total += rsb[h, i]
        piece[h] = total

        @pl.when(xh == 1)
        def _():
            gather(h, 0).start()

        for i in range(1, 2 * NZ):
            gather(h, i).start()

        @pl.when(xh == 0)
        def _():
            s[h, c, :, my_lanes] = piece[h]

    scatter_half(0)
    pl.semaphore_wait(ready, 1)
    gather_half(0)
    scatter_half(1)

    for w in range(WIN):
        at = (1 - y // 2) * WIN + w
        exchange(w).wait_recv()
        columns = ab[at, PAD : PAD + W, 0:128].astype(F32)
        fill_second_lane_half(ab, at, columns)
        fill_edges(re32, at, columns[:PAD], columns[W - PAD :])
    re[...] = re32[...].astype(BF16)

    def gathered(h):
        @pl.when(xh == 1)
        def _():
            gather(h, 0).wait_recv()

        for i in range(1, 2 * NZ):
            gather(h, i).wait_recv()

    def sent(h):
        @pl.when(xh == 1)
        def _():
            gather(h, 0).wait_send()

        lax.fori_loop(1, 2 * NZ, run(lambda i: gather(h, i).wait_send()), 0)
        lax.fori_loop(1, 2 * NZ, run(lambda i: scatter(h, i).wait_send()), 0)
        for j in range(2):
            merge(2 * h + j).wait_send()
        swap(h).wait_send()

    lane = lax.broadcasted_iota(jnp.int32, (16, 128), 1)

    def expand(h, k):
        def window(w, ext):
            at = pl.ds(pl.multiple_of(w * W, W), W)
            x = s[h, k, :, at].astype(F32)
            results = []
            for f in range(FINE):
                shift = f - 2
                rows = pl.ds(pl.multiple_of(k * 128 + f * 16, 16), 16)
                moved = shifted_rows(x, shift)
                if shift > 0:
                    wraps, tile = lane < shift, 0
                else:
                    wraps, tile = lane >= 128 + shift, W - 128
                edge = moved[:, tile : tile + 128]
                kept = jnp.where(wraps, 0.0, edge)
                if tile == 0:
                    moved = jnp.concatenate([kept, moved[:, 128:]], 1)
                else:
                    moved = jnp.concatenate([moved[:, :tile], kept], 1)
                lhs[h, rows, at] = moved.astype(BF16)
                lost = jnp.where(wraps, edge, 0.0)
                results.append(ext[f] + pltpu.roll(lost, w * 8 + 2, 1))
            return tuple(results)

        ext = lax.fori_loop(0, 2 * WIN, window, tuple(jnp.zeros((16, 128), F32) for _ in range(FINE)))
        for f in range(FINE):
            lext[h, pl.ds(pl.multiple_of(k * 128 + f * 16, 16), 16), :] = ext[f].astype(BF16)

    def correlate(h, p, lanes):
        acc = jnp.dot(lext[h], re[p, :, :lanes], preferred_element_type=F32)
        for w in range(2 * WIN):
            acc += jnp.dot(
                lhs[h, :, w * W : (w + 1) * W],
                ab[w, pl.ds(pl.multiple_of(p * 16, 16), W), 0:lanes],
                preferred_element_type=F32,
            )
        return acc

    def y_copy(k, p, lanes):
        return pltpu.make_async_remote_copy(
            src_ref=ysnd.at[k, p, :, pl.ds(0, lanes)], dst_ref=yrcv.at[k, p, :, pl.ds(0, lanes)],
            send_sem=y_s.at[k, p], recv_sem=y_r.at[k, p],
            device_id=device(z, xh, c, (y + 3 + 2 * k) % NY, xl), device_id_type=MESH,
        )

    def x_copy(p, lanes):
        return pltpu.make_async_remote_copy(
            src_ref=xsnd.at[p, :, pl.ds(0, lanes)], dst_ref=xrcv.at[p, :, pl.ds(0, lanes)],
            send_sem=x_s.at[p], recv_sem=x_r.at[p],
            device_id=device(z, xh, c, y, 1 - xl), device_id_type=MESH,
        )

    def first(p, lanes=256):
        acc = correlate(0, p, lanes)
        for k in range(2):
            ysnd[k, p, :, :lanes] = acc[128 * k : 128 * k + 128].astype(BF16)
            y_copy(k, p, lanes).start()

    def second(p, lanes=256):
        acc = correlate(1, p, lanes)
        mine, other = [], []
        for k in range(2):
            y_copy(k, p, lanes).wait_recv()
            both = acc[128 * k : 128 * k + 128] + yrcv[k, p, :, :lanes].astype(F32)
            both = both.reshape(FINE, 2, 8, lanes)
            low, high = both[:, 0].reshape(64, lanes), both[:, 1].reshape(64, lanes)
            mine.append(jnp.where(xl == 0, low, high))
            other.append(jnp.where(xl == 0, high, low))
        own[p, :, :lanes] = jnp.concatenate(mine, 0)
        xsnd[p, :, :lanes] = jnp.concatenate(other, 0).astype(BF16)
        x_copy(p, lanes).start()

    def finish(p, lanes=256):
        x_copy(p, lanes).wait_recv()
        acc = (own[p, :, :lanes] + xrcv[p, :, :lanes].astype(F32)) * WEIGHT
        for g in range(lanes // 128):
            out[2 * p + g] = acc[:, 128 * g : 128 * g + 128]

    gathered(0)
    swap(0).start()
    gather_half(1)
    expand(0, c)
    swap(0).wait_recv()
    expand(0, 1 - c)
    lax.fori_loop(0, PAIRS - 1, run(first), 0)
    gathered(1)
    swap(1).start()
    first(PAIRS - 1, 128)
    expand(1, c)
    swap(1).wait_recv()
    expand(1, 1 - c)
    lax.fori_loop(0, PAIRS - 1, run(second), 0)
    second(PAIRS - 1, 128)

    for h in range(2):
        sent(h)
    for w in range(WIN):
        exchange(w).wait_send()

    def all_sent(p, lanes=256):
        for k in range(2):
            y_copy(k, p, lanes).wait_send()
        x_copy(p, lanes).wait_send()

    lax.fori_loop(0, PAIRS - 1, run(all_sent), 0)
    all_sent(PAIRS - 1, 128)
    lax.fori_loop(0, PAIRS - 1, run(finish), 0)
    finish(PAIRS - 1, 128)


def on_device(records, source_block, quality):
    vmem = pl.BlockSpec(memory_space=pltpu.VMEM)
    dma = pltpu.SemaphoreType.DMA
    sums = pl.pallas_call(
        kernel,
        out_shape=jax.ShapeDtypeStruct((COARSE, 128, 128), F32),
        in_specs=[vmem, pl.BlockSpec(memory_space=pltpu.SMEM), vmem],
        out_specs=vmem,
        scratch_shapes=[
            pltpu.VMEM((128, SHARE), F32),
            pltpu.VMEM((2, NY, 16, SHARE), BF16),
            pltpu.VMEM((NY, 16, SHARE), BF16),
            pltpu.VMEM((2, 2 * NZ, 16, PIECE), BF16),
            pltpu.VMEM((2, 16, PIECE), BF16),
            pltpu.VMEM((2, 2, 16, 2 * SHARE), BF16),
            pltpu.VMEM((2 * WIN, ROWS, 256), BF16),
            pltpu.VMEM((PAIRS, 128, 256), F32),
            pltpu.VMEM((PAIRS, 128, 256), BF16),
            pltpu.VMEM((2, 256, 2 * SHARE), BF16),
            pltpu.VMEM((2, 256, 128), BF16),
            pltpu.VMEM((PAIRS, 128, 256), F32),
            pltpu.VMEM((2, PAIRS, 128, 256), BF16),
            pltpu.VMEM((2, PAIRS, 128, 256), BF16),
            pltpu.VMEM((PAIRS, 128, 256), BF16),
            pltpu.VMEM((PAIRS, 128, 256), BF16),
            dma((NY,)), dma((NY,)), dma((2, 2 * NZ)), dma((2, 2 * NZ)), dma((2, 2 * NZ)), dma((2, 2 * NZ)),
            dma((WIN,)), dma((WIN,)), dma((2,)), dma((2,)),
            dma((2, PAIRS)), dma((2, PAIRS)), dma((PAIRS,)), dma((PAIRS,)),
            pltpu.SemaphoreType.REGULAR,
        ],
        compiler_params=pltpu.CompilerParams(
            collective_id=0, has_side_effects=True, vmem_limit_bytes=56 << 20
        ),
        name="correlate",
    )(records, source_block, quality.reshape(1, 128))
    stacks = sums.reshape(COARSE, 2, FINE, 8, 128).transpose(1, 3, 0, 2, 4)
    return stacks.reshape(2, 8, COARSE * FINE, 128)[:, :, :LAGS]


def solution(mesh):
    in_specs = (P("rx", "tm"), P(), P("rx"))
    out_specs = P(None, "tm", None, "rx")
    return jax.shard_map(
        on_device, mesh=mesh, in_specs=in_specs, out_specs=out_specs, check_vma=False
    )
```

```python
import math

import jax
import jax.numpy as jnp
from jax import lax
from jax.experimental import pallas as pl
from jax.experimental.pallas import tpu as pltpu
from jax.sharding import PartitionSpec as P

W = 1024
LAGS = 101
FINE = 8
COARSE = 13
PAD = 48
NZ = 8
NY = 4
WIN = 3
ROWS = W + 2 * PAD
SHARE = WIN * W
PIECE = SHARE // NZ
PAIRS = (COARSE + 1) // 2
WEIGHT = 1.0 / math.sqrt(24 * W)
MESH = pl.DeviceIdType.MESH
F32 = jnp.float32
BF16 = jnp.bfloat16


def device(z, xh, c, y, xl):
    return ((z * 2 + xh) * 2 + c, y * 2 + xl)


def shifted_rows(values, shift):
    return pltpu.roll(values, shift % values.shape[1], 1)


def fill_second_lane_half(ab, w, columns):
    zeros = jnp.zeros((8, 128), F32)
    ab[w, PAD - 16 : PAD + W, 128:256] = jnp.concatenate([zeros, columns, zeros], 0).astype(BF16)


def edge_rows(block, keep_low):
    blocks = block.reshape(PAD // 8, 8, 128)
    rolled = pltpu.roll(blocks, 2, 1)
    row = lax.broadcasted_iota(jnp.int32, rolled.shape, 1)
    keep = row < 2 if keep_low else row >= 2
    return jnp.where(keep, rolled, 0.0)


def fill_edges(re32, w, head, tail):
    low = edge_rows(head, True)
    high = edge_rows(tail, False)
    at = pl.ds(pl.multiple_of(w * 8, 8), 8)
    for m in range(1, PAD // 8 + 1):
        c = 6 + m
        re32[c // 2, at, (c % 2) * 128 : (c % 2) * 128 + 128] = low[m - 1]
        c = 6 - m
        re32[c // 2, at, (c % 2) * 128 : (c % 2) * 128 + 128] = high[PAD // 8 - m]


def kernel(
    rec_hbm, blk, qual, out,
    rec,     wh, v, mrg, rsb, piece, s, ab, re32, re, lhs, lext, own, ysnd, yrcv, xsnd, xrcv,
    mrg_s, mrg_r, rs_s, rs_r, ag_s, ag_r, ex_s, ex_r, cx_s, cx_r, y_s, y_r, x_s, x_r, ready, rec_sem,
):
    rx = lax.axis_index("rx")
    tm = lax.axis_index("tm")
    z, xh, c = rx // 4, (rx // 2) % 2, rx % 2
    y, xl = tm // 2, tm % 2
    sibling = device(z, xh, 1 - c, y, xl)

    def plane_peer(i):
        return (z + i // 2) % NZ, (xh + i % 2) % 2

    def run(fn):
        def step(i, _):
            fn(i)
            return 0

        return step

    barrier = pltpu.get_barrier_semaphore()

    def greet(peer):
        pl.semaphore_signal(barrier, inc=1, device_id=peer, device_id_type=MESH)

    greet(sibling)
    lax.fori_loop(1, 2 * NZ, run(lambda i: greet(device(*plane_peer(i), c, y, xl))), 0)
    for g in range(1, NY):
        greet(device(z, xh, c, (y + g) % NY, xl))
    greet(device(z, xh, c, y, 1 - xl))

    def load(w):
        at = pl.ds(w * W, W)
        return pltpu.make_async_copy(rec_hbm.at[:, at], rec.at[:, at], rec_sem.at[w])

    for w in range(WIN):
        load(w).start()

    ones = jnp.broadcast_to(qual[...].astype(F32), (128, 128))
    usable = jnp.transpose(ones)[:, :1]
    marks = []
    for k in range(2):
        b = blk[k]
        for half in range(2):
            marks.append((b == rx * 2 + half).astype(F32))
    for w in range(WIN):
        load(w).wait()
        x = rec[:, w * W : (w + 1) * W]
        power = jnp.sum(x * x, axis=1, keepdims=True) * (1.0 / W)
        white = x * (lax.rsqrt(power + 1e-06) * usable)
        wh[:, w * W : (w + 1) * W] = white
        for k in range(2):
            rows = white[:64] * marks[2 * k] + white[64:] * marks[2 * k + 1]
            v[k, :, :, w * W : (w + 1) * W] = rows.astype(BF16).reshape(NY, 16, W)

    zero_rows = jnp.zeros((PAD, 256), BF16)
    for w in range(2 * WIN):
        ab[w, 0:PAD, :] = zero_rows
        ab[w, PAD + W : ROWS, :] = zero_rows
    re32[...] = jnp.zeros_like(re32)
    for w in range(WIN):
        columns = jnp.transpose(wh[:, w * W : (w + 1) * W]).astype(BF16)
        at = (y // 2) * WIN + w
        ab[at, PAD : PAD + W, 0:128] = columns
        columns = columns.astype(F32)
        fill_second_lane_half(ab, at, columns)
        fill_edges(re32, at, columns[:PAD], columns[W - PAD :])

    pl.semaphore_wait(barrier, 1 + (2 * NZ - 1) + NY)
    pl.semaphore_signal(ready, inc=1, device_id=device(z, xh, c, (y + 2) % NY, xl), device_id_type=MESH)

    def merge(j):
        yd = (y + 1 + 2 * j + j // 2) % NY
        return pltpu.make_async_remote_copy(
            src_ref=v.at[1 - c, yd], dst_ref=mrg.at[yd], send_sem=mrg_s.at[j], recv_sem=mrg_r.at[j],
            device_id=sibling, device_id_type=MESH,
        )

    def exchange(w):
        slot = ab.at[(y // 2) * WIN + w, pl.ds(PAD, W), pl.ds(0, 128)]
        return pltpu.make_async_remote_copy(
            src_ref=slot, dst_ref=slot, send_sem=ex_s.at[w], recv_sem=ex_r.at[w],
            device_id=device(z, xh, c, (y + 2) % NY, xl), device_id_type=MESH,
        )

    def group_of(h, xd):
        if h == 0:
            return (y + 3 + 2 * ((c + xd) % 2)) % NY
        return (y + 2 * xd) % NY

    def scatter(h, i):
        pz, pxh = plane_peer(i)
        return pltpu.make_async_remote_copy(
            src_ref=v.at[c, group_of(h, pxh), :, pl.ds(pl.multiple_of(pz * PIECE, 128), PIECE)],
            dst_ref=rsb.at[h, i], send_sem=rs_s.at[h, i], recv_sem=rs_r.at[h, i],
            device_id=device(pz, pxh, c, y, xl), device_id_type=MESH,
        )

    my_lanes = pl.ds(pl.multiple_of((y // 2) * SHARE + z * PIECE, 128), PIECE)

    def gather(h, i):
        return pltpu.make_async_remote_copy(
            src_ref=piece.at[h], dst_ref=s.at[h, c, :, my_lanes],
            send_sem=ag_s.at[h, i], recv_sem=ag_r.at[h, i],
            device_id=device(*plane_peer(i), c, (y + 2 * xh) % NY, xl), device_id_type=MESH,
        )

    def swap(h):
        return pltpu.make_async_remote_copy(
            src_ref=s.at[h, c], dst_ref=s.at[h, c], send_sem=cx_s.at[h], recv_sem=cx_r.at[h],
            device_id=sibling, device_id_type=MESH,
        )

    for j in range(NY):
        merge(j).start()
    for w in range(WIN):
        exchange(w).start()
    def scatter_half(h):
        for j in range(2):
            merge(2 * h + j).wait_recv()
            yd = (y + 1 + 2 * j + h) % NY
            v[c, yd] = v[c, yd] + mrg[yd]
        for i in range(1, 2 * NZ):
            scatter(h, i).start()

    def gather_half(h):
        total = v[c, group_of(h, xh), :, pl.ds(pl.multiple_of(z * PIECE, 128), PIECE)]
        for i in range(1, 2 * NZ):
            scatter(h, i).wait_recv()
            total += rsb[h, i]
        piece[h] = total

        @pl.when(xh == 1)
        def _():
            gather(h, 0).start()

        for i in range(1, 2 * NZ):
            gather(h, i).start()

        @pl.when(xh == 0)
        def _():
            s[h, c, :, my_lanes] = piece[h]

    scatter_half(0)
    pl.semaphore_wait(ready, 1)
    gather_half(0)
    scatter_half(1)

    for w in range(WIN):
        at = (1 - y // 2) * WIN + w
        exchange(w).wait_recv()
        columns = ab[at, PAD : PAD + W, 0:128].astype(F32)
        fill_second_lane_half(ab, at, columns)
        fill_edges(re32, at, columns[:PAD], columns[W - PAD :])
    re[...] = re32[...].astype(BF16)

    def gathered(h):
        @pl.when(xh == 1)
        def _():
            gather(h, 0).wait_recv()

        for i in range(1, 2 * NZ):
            gather(h, i).wait_recv()

    def sent(h):
        @pl.when(xh == 1)
        def _():
            gather(h, 0).wait_send()

        lax.fori_loop(1, 2 * NZ, run(lambda i: gather(h, i).wait_send()), 0)
        lax.fori_loop(1, 2 * NZ, run(lambda i: scatter(h, i).wait_send()), 0)
        for j in range(2):
            merge(2 * h + j).wait_send()
        swap(h).wait_send()

    lane = lax.broadcasted_iota(jnp.int32, (16, 128), 1)

    def expand(h, k):
        def window(w, ext):
            at = pl.ds(pl.multiple_of(w * W, W), W)
            x = s[h, k, :, at].astype(F32)
            results = []
            for f in range(FINE):
                shift = f - 2
                rows = pl.ds(pl.multiple_of(k * 128 + f * 16, 16), 16)
                moved = shifted_rows(x, shift)
                if shift > 0:
                    wraps, tile = lane < shift, 0
                else:
                    wraps, tile = lane >= 128 + shift, W - 128
                edge = moved[:, tile : tile + 128]
                kept = jnp.where(wraps, 0.0, edge)
                if tile == 0:
                    moved = jnp.concatenate([kept, moved[:, 128:]], 1)
                else:
                    moved = jnp.concatenate([moved[:, :tile], kept], 1)
                lhs[h, rows, at] = moved.astype(BF16)
                lost = jnp.where(wraps, edge, 0.0)
                results.append(ext[f] + pltpu.roll(lost, w * 8 + 2, 1))
            return tuple(results)

        ext = lax.fori_loop(0, 2 * WIN, window, tuple(jnp.zeros((16, 128), F32) for _ in range(FINE)))
        for f in range(FINE):
            lext[h, pl.ds(pl.multiple_of(k * 128 + f * 16, 16), 16), :] = ext[f].astype(BF16)

    def correlate(h, p, lanes):
        acc = jnp.dot(lext[h], re[p, :, :lanes], preferred_element_type=F32)
        for w in range(2 * WIN):
            acc += jnp.dot(
                lhs[h, :, w * W : (w + 1) * W],
                ab[w, pl.ds(pl.multiple_of(p * 16, 16), W), 0:lanes],
                preferred_element_type=F32,
            )
        return acc

    def y_copy(k, p, lanes):
        return pltpu.make_async_remote_copy(
            src_ref=ysnd.at[k, p, :, pl.ds(0, lanes)], dst_ref=yrcv.at[k, p, :, pl.ds(0, lanes)],
            send_sem=y_s.at[k, p], recv_sem=y_r.at[k, p],
            device_id=device(z, xh, c, (y + 3 + 2 * k) % NY, xl), device_id_type=MESH,
        )

    def x_copy(p, lanes):
        return pltpu.make_async_remote_copy(
            src_ref=xsnd.at[p, :, pl.ds(0, lanes)], dst_ref=xrcv.at[p, :, pl.ds(0, lanes)],
            send_sem=x_s.at[p], recv_sem=x_r.at[p],
            device_id=device(z, xh, c, y, 1 - xl), device_id_type=MESH,
        )

    def first(p, lanes=256):
        acc = correlate(0, p, lanes)
        for k in range(2):
            ysnd[k, p, :, :lanes] = acc[128 * k : 128 * k + 128].astype(BF16)
            y_copy(k, p, lanes).start()

    def second(p, lanes=256):
        acc = correlate(1, p, lanes)
        mine, other = [], []
        for k in range(2):
            y_copy(k, p, lanes).wait_recv()
            both = acc[128 * k : 128 * k + 128] + yrcv[k, p, :, :lanes].astype(F32)
            both = both.reshape(FINE, 2, 8, lanes)
            low, high = both[:, 0].reshape(64, lanes), both[:, 1].reshape(64, lanes)
            mine.append(jnp.where(xl == 0, low, high))
            other.append(jnp.where(xl == 0, high, low))
        own[p, :, :lanes] = jnp.concatenate(mine, 0)
        xsnd[p, :, :lanes] = jnp.concatenate(other, 0).astype(BF16)
        x_copy(p, lanes).start()

    def finish(p, lanes=256):
        x_copy(p, lanes).wait_recv()
        acc = (own[p, :, :lanes] + xrcv[p, :, :lanes].astype(F32)) * WEIGHT
        for g in range(lanes // 128):
            out[2 * p + g] = acc[:, 128 * g : 128 * g + 128]

    gathered(0)
    swap(0).start()
    gather_half(1)
    expand(0, c)
    swap(0).wait_recv()
    expand(0, 1 - c)
    lax.fori_loop(0, PAIRS - 1, run(first), 0)
    gathered(1)
    swap(1).start()
    first(PAIRS - 1, 128)
    expand(1, c)
    swap(1).wait_recv()
    expand(1, 1 - c)
    lax.fori_loop(0, PAIRS - 1, run(second), 0)
    second(PAIRS - 1, 128)

    for h in range(2):
        sent(h)
    for w in range(WIN):
        exchange(w).wait_send()

    def all_sent(p, lanes=256):
        for k in range(2):
            y_copy(k, p, lanes).wait_send()
        x_copy(p, lanes).wait_send()

    lax.fori_loop(0, PAIRS - 1, run(all_sent), 0)
    all_sent(PAIRS - 1, 128)
    lax.fori_loop(0, PAIRS - 1, run(finish), 0)
    finish(PAIRS - 1, 128)


def on_device(records, source_block, quality):
    vmem = pl.BlockSpec(memory_space=pltpu.VMEM)
    dma = pltpu.SemaphoreType.DMA
    sums = pl.pallas_call(
        kernel,
        out_shape=jax.ShapeDtypeStruct((COARSE, 128, 128), F32),
        in_specs=[pl.BlockSpec(memory_space=pl.ANY), pl.BlockSpec(memory_space=pltpu.SMEM), vmem],
        out_specs=vmem,
        scratch_shapes=[
            pltpu.VMEM((128, SHARE), F32),
            pltpu.VMEM((128, SHARE), F32),
            pltpu.VMEM((2, NY, 16, SHARE), BF16),
            pltpu.VMEM((NY, 16, SHARE), BF16),
            pltpu.VMEM((2, 2 * NZ, 16, PIECE), BF16),
            pltpu.VMEM((2, 16, PIECE), BF16),
            pltpu.VMEM((2, 2, 16, 2 * SHARE), BF16),
            pltpu.VMEM((2 * WIN, ROWS, 256), BF16),
            pltpu.VMEM((PAIRS, 128, 256), F32),
            pltpu.VMEM((PAIRS, 128, 256), BF16),
            pltpu.VMEM((2, 256, 2 * SHARE), BF16),
            pltpu.VMEM((2, 256, 128), BF16),
            pltpu.VMEM((PAIRS, 128, 256), F32),
            pltpu.VMEM((2, PAIRS, 128, 256), BF16),
            pltpu.VMEM((2, PAIRS, 128, 256), BF16),
            pltpu.VMEM((PAIRS, 128, 256), BF16),
            pltpu.VMEM((PAIRS, 128, 256), BF16),
            dma((NY,)), dma((NY,)), dma((2, 2 * NZ)), dma((2, 2 * NZ)), dma((2, 2 * NZ)), dma((2, 2 * NZ)),
            dma((WIN,)), dma((WIN,)), dma((2,)), dma((2,)),
            dma((2, PAIRS)), dma((2, PAIRS)), dma((PAIRS,)), dma((PAIRS,)),
            pltpu.SemaphoreType.REGULAR, dma((WIN,)),
        ],
        compiler_params=pltpu.CompilerParams(
            collective_id=0, has_side_effects=True, vmem_limit_bytes=56 << 20
        ),
        name="correlate",
    )(records, source_block, quality.reshape(1, 128))
    stacks = sums.reshape(COARSE, 2, FINE, 8, 128).transpose(1, 3, 0, 2, 4)
    return stacks.reshape(2, 8, COARSE * FINE, 128)[:, :, :LAGS]


def solution(mesh):
    in_specs = (P("rx", "tm"), P(), P("rx"))
    out_specs = P(None, "tm", None, "rx")
    return jax.shard_map(
        on_device, mesh=mesh, in_specs=in_specs, out_specs=out_specs, check_vma=False
    )
```

```python
import math

import jax
import jax.numpy as jnp
from jax import lax
from jax.experimental import pallas as pl
from jax.experimental.pallas import tpu as pltpu
from jax.sharding import PartitionSpec as P

W = 1024
LAGS = 101
FINE = 8
COARSE = 13
PAD = 48
NZ = 8
NY = 4
WIN = 3
ROWS = W + 2 * PAD
SHARE = WIN * W
PIECE = SHARE // NZ
PAIRS = (COARSE + 1) // 2
WEIGHT = 1.0 / math.sqrt(24 * W)
MESH = pl.DeviceIdType.MESH
F32 = jnp.float32
BF16 = jnp.bfloat16


def device(z, xh, c, y, xl):
    return ((z * 2 + xh) * 2 + c, y * 2 + xl)


def shifted_rows(values, shift):
    return pltpu.roll(values, shift % values.shape[1], 1)


def fill_second_lane_half(ab, w, columns):
    zeros = jnp.zeros((8, 128), F32)
    ab[w, PAD - 16 : PAD + W, 128:256] = jnp.concatenate([zeros, columns, zeros], 0).astype(BF16)


def edge_rows(block, keep_low):
    blocks = block.reshape(PAD // 8, 8, 128)
    rolled = pltpu.roll(blocks, 2, 1)
    row = lax.broadcasted_iota(jnp.int32, rolled.shape, 1)
    keep = row < 2 if keep_low else row >= 2
    return jnp.where(keep, rolled, 0.0)


def fill_edges(re32, w, head, tail):
    low = edge_rows(head, True)
    high = edge_rows(tail, False)
    at = pl.ds(pl.multiple_of(w * 8, 8), 8)
    for m in range(1, PAD // 8 + 1):
        c = 6 + m
        re32[c // 2, at, (c % 2) * 128 : (c % 2) * 128 + 128] = low[m - 1]
        c = 6 - m
        re32[c // 2, at, (c % 2) * 128 : (c % 2) * 128 + 128] = high[PAD // 8 - m]


def kernel(
    rec_hbm, blk, qual, out,
    rec,     wh, v, mrg, rsb, piece, s, ab, re32, re, lhs, lext, own, ysnd, yrcv, xsnd, xrcv,
    mrg_s, mrg_r, rs_s, rs_r, ag_s, ag_r, ex_s, ex_r, cx_s, cx_r, y_s, y_r, x_s, x_r, ready, rec_sem,
):
    rx = lax.axis_index("rx")
    tm = lax.axis_index("tm")
    z, xh, c = rx // 4, (rx // 2) % 2, rx % 2
    y, xl = tm // 2, tm % 2
    sibling = device(z, xh, 1 - c, y, xl)

    def plane_peer(i):
        return (z + i // 2) % NZ, (xh + i % 2) % 2

    def run(fn):
        def step(i, _):
            fn(i)
            return 0

        return step

    barrier = pltpu.get_barrier_semaphore()

    def greet(peer):
        pl.semaphore_signal(barrier, inc=1, device_id=peer, device_id_type=MESH)

    greet(sibling)
    lax.fori_loop(1, 2 * NZ, run(lambda i: greet(device(*plane_peer(i), c, y, xl))), 0)
    for g in range(1, NY):
        greet(device(z, xh, c, (y + g) % NY, xl))
    greet(device(z, xh, c, y, 1 - xl))

    def load(w):
        at = pl.ds(w * W, W)
        return pltpu.make_async_copy(rec_hbm.at[:, at], rec.at[:, at], rec_sem.at[w])

    for w in range(WIN):
        load(w).start()

    ones = jnp.broadcast_to(qual[...].astype(F32), (128, 128))
    usable = jnp.transpose(ones)[:, :1]
    marks = []
    for k in range(2):
        b = blk[k]
        for half in range(2):
            marks.append((b == rx * 2 + half).astype(F32))
    for w in range(WIN):
        load(w).wait()
        x = rec[:, w * W : (w + 1) * W]
        power = jnp.sum(x * x, axis=1, keepdims=True) * (1.0 / W)
        white = x * (lax.rsqrt(power + 1e-06) * usable)
        wh[:, w * W : (w + 1) * W] = white
        for k in range(2):
            rows = white[:64] * marks[2 * k] + white[64:] * marks[2 * k + 1]
            v[k, :, :, w * W : (w + 1) * W] = rows.astype(BF16).reshape(NY, 16, W)

    zero_rows = jnp.zeros((PAD, 256), BF16)
    for w in range(2 * WIN):
        ab[w, 0:PAD, :] = zero_rows
        ab[w, PAD + W : ROWS, :] = zero_rows
    re32[...] = jnp.zeros_like(re32)
    for w in range(WIN):
        columns = jnp.transpose(wh[:, w * W : (w + 1) * W]).astype(BF16)
        at = (y // 2) * WIN + w
        ab[at, PAD : PAD + W, 0:128] = columns
        columns = columns.astype(F32)
        fill_second_lane_half(ab, at, columns)
        fill_edges(re32, at, columns[:PAD], columns[W - PAD :])

    pl.semaphore_wait(barrier, 1 + (2 * NZ - 1) + NY)
    pl.semaphore_signal(ready, inc=1, device_id=device(z, xh, c, (y + 2) % NY, xl), device_id_type=MESH)

    def merge(j):
        yd = (y + 1 + 2 * j + j // 2) % NY
        return pltpu.make_async_remote_copy(
            src_ref=v.at[1 - c, yd], dst_ref=mrg.at[yd], send_sem=mrg_s.at[j], recv_sem=mrg_r.at[j],
            device_id=sibling, device_id_type=MESH,
        )

    def exchange(w):
        slot = ab.at[(y // 2) * WIN + w, pl.ds(PAD, W), pl.ds(0, 128)]
        return pltpu.make_async_remote_copy(
            src_ref=slot, dst_ref=slot, send_sem=ex_s.at[w], recv_sem=ex_r.at[w],
            device_id=device(z, xh, c, (y + 2) % NY, xl), device_id_type=MESH,
        )

    def group_of(h, xd):
        if h == 0:
            return (y + 3 + 2 * ((c + xd) % 2)) % NY
        return (y + 2 * xd) % NY

    def scatter(h, i):
        pz, pxh = plane_peer(i)
        return pltpu.make_async_remote_copy(
            src_ref=v.at[c, group_of(h, pxh), :, pl.ds(pl.multiple_of(pz * PIECE, 128), PIECE)],
            dst_ref=rsb.at[h, i], send_sem=rs_s.at[h, i], recv_sem=rs_r.at[h, i],
            device_id=device(pz, pxh, c, y, xl), device_id_type=MESH,
        )

    my_lanes = pl.ds(pl.multiple_of((y // 2) * SHARE + z * PIECE, 128), PIECE)

    def gather(h, i):
        return pltpu.make_async_remote_copy(
            src_ref=piece.at[h], dst_ref=s.at[h, c, :, my_lanes],
            send_sem=ag_s.at[h, i], recv_sem=ag_r.at[h, i],
            device_id=device(*plane_peer(i), c, (y + 2 * xh) % NY, xl), device_id_type=MESH,
        )

    def swap(h):
        return pltpu.make_async_remote_copy(
            src_ref=s.at[h, c], dst_ref=s.at[h, c], send_sem=cx_s.at[h], recv_sem=cx_r.at[h],
            device_id=sibling, device_id_type=MESH,
        )

    for j in range(NY):
        merge(j).start()
    for w in range(WIN):
        exchange(w).start()
    def scatter_half(h):
        for j in range(2):
            merge(2 * h + j).wait_recv()
            yd = (y + 1 + 2 * j + h) % NY
            v[c, yd] = v[c, yd] + mrg[yd]
        for i in range(1, 2 * NZ):
            scatter(h, i).start()

    def gather_half(h):
        total = v[c, group_of(h, xh), :, pl.ds(pl.multiple_of(z * PIECE, 128), PIECE)]
        for i in range(1, 2 * NZ):
            scatter(h, i).wait_recv()
            total += rsb[h, i]
        piece[h] = total

        @pl.when(xh == 1)
        def _():
            gather(h, 0).start()

        for i in range(1, 2 * NZ):
            gather(h, i).start()

        @pl.when(xh == 0)
        def _():
            s[h, c, :, my_lanes] = piece[h]

    scatter_half(0)
    pl.semaphore_wait(ready, 1)
    gather_half(0)
    scatter_half(1)

    for w in range(WIN):
        at = (1 - y // 2) * WIN + w
        exchange(w).wait_recv()
        columns = ab[at, PAD : PAD + W, 0:128].astype(F32)
        fill_second_lane_half(ab, at, columns)
        fill_edges(re32, at, columns[:PAD], columns[W - PAD :])
    re[...] = re32[...].astype(BF16)

    def gathered(h):
        @pl.when(xh == 1)
        def _():
            gather(h, 0).wait_recv()

        for i in range(1, 2 * NZ):
            gather(h, i).wait_recv()

    def sent(h):
        @pl.when(xh == 1)
        def _():
            gather(h, 0).wait_send()

        lax.fori_loop(1, 2 * NZ, run(lambda i: gather(h, i).wait_send()), 0)
        lax.fori_loop(1, 2 * NZ, run(lambda i: scatter(h, i).wait_send()), 0)
        for j in range(2):
            merge(2 * h + j).wait_send()
        swap(h).wait_send()

    lane = lax.broadcasted_iota(jnp.int32, (16, 128), 1)

    def expand(h, k):
        def window(w, ext):
            at = pl.ds(pl.multiple_of(w * W, W), W)
            x = s[h, k, :, at].astype(F32)
            results = []
            for f in range(FINE):
                shift = f - 2
                rows = pl.ds(pl.multiple_of(k * 128 + f * 16, 16), 16)
                moved = shifted_rows(x, shift)
                if shift > 0:
                    wraps, tile = lane < shift, 0
                else:
                    wraps, tile = lane >= 128 + shift, W - 128
                edge = moved[:, tile : tile + 128]
                kept = jnp.where(wraps, 0.0, edge)
                if tile == 0:
                    moved = jnp.concatenate([kept, moved[:, 128:]], 1)
                else:
                    moved = jnp.concatenate([moved[:, :tile], kept], 1)
                lhs[h, rows, at] = moved.astype(BF16)
                lost = jnp.where(wraps, edge, 0.0)
                results.append(ext[f] + pltpu.roll(lost, w * 8 + 2, 1))
            return tuple(results)

        ext = lax.fori_loop(0, 2 * WIN, window, tuple(jnp.zeros((16, 128), F32) for _ in range(FINE)))
        for f in range(FINE):
            lext[h, pl.ds(pl.multiple_of(k * 128 + f * 16, 16), 16), :] = ext[f].astype(BF16)

    def correlate(h, p, lanes):
        acc = jnp.dot(lext[h], re[p, :, :lanes], preferred_element_type=F32)
        for w in range(2 * WIN):
            acc += jnp.dot(
                lhs[h, :, w * W : (w + 1) * W],
                ab[w, pl.ds(pl.multiple_of(p * 16, 16), W), 0:lanes],
                preferred_element_type=F32,
            )
        return acc

    def y_copy(k, p, lanes):
        return pltpu.make_async_remote_copy(
            src_ref=ysnd.at[k, p, :, pl.ds(0, lanes)], dst_ref=yrcv.at[k, p, :, pl.ds(0, lanes)],
            send_sem=y_s.at[k, p], recv_sem=y_r.at[k, p],
            device_id=device(z, xh, c, (y + 3 + 2 * k) % NY, xl), device_id_type=MESH,
        )

    def x_copy(p, lanes):
        return pltpu.make_async_remote_copy(
            src_ref=xsnd.at[p, :, pl.ds(0, lanes)], dst_ref=xrcv.at[p, :, pl.ds(0, lanes)],
            send_sem=x_s.at[p], recv_sem=x_r.at[p],
            device_id=device(z, xh, c, y, 1 - xl), device_id_type=MESH,
        )

    def first(p, lanes=256):
        acc = correlate(0, p, lanes)
        for k in range(2):
            ysnd[k, p, :, :lanes] = acc[128 * k : 128 * k + 128].astype(BF16)
            y_copy(k, p, lanes).start()

    def second(p, lanes=256):
        acc = correlate(1, p, lanes)
        mine, other = [], []
        for k in range(2):
            y_copy(k, p, lanes).wait_recv()
            both = acc[128 * k : 128 * k + 128] + yrcv[k, p, :, :lanes].astype(F32)
            both = both.reshape(FINE, 2, 8, lanes)
            low, high = both[:, 0].reshape(64, lanes), both[:, 1].reshape(64, lanes)
            mine.append(jnp.where(xl == 0, low, high))
            other.append(jnp.where(xl == 0, high, low))
        own[p, :, :lanes] = jnp.concatenate(mine, 0)
        xsnd[p, :, :lanes] = jnp.concatenate(other, 0).astype(BF16)
        x_copy(p, lanes).start()

    def finish(p, lanes=256):
        x_copy(p, lanes).wait_recv()
        acc = (own[p, :, :lanes] + xrcv[p, :, :lanes].astype(F32)) * WEIGHT
        for g in range(lanes // 128):
            out[2 * p + g] = acc[:, 128 * g : 128 * g + 128]

    gathered(0)
    swap(0).start()
    expand(0, c)
    gather_half(1)
    swap(0).wait_recv()
    expand(0, 1 - c)
    lax.fori_loop(0, PAIRS - 1, run(first), 0)
    gathered(1)
    swap(1).start()
    first(PAIRS - 1, 128)
    expand(1, c)
    swap(1).wait_recv()
    expand(1, 1 - c)
    lax.fori_loop(0, PAIRS - 1, run(second), 0)
    second(PAIRS - 1, 128)

    lax.fori_loop(0, PAIRS - 1, run(finish), 0)
    finish(PAIRS - 1, 128)

    for h in range(2):
        sent(h)
    for w in range(WIN):
        exchange(w).wait_send()

    def all_sent(p, lanes=256):
        for k in range(2):
            y_copy(k, p, lanes).wait_send()
        x_copy(p, lanes).wait_send()

    lax.fori_loop(0, PAIRS - 1, run(all_sent), 0)
    all_sent(PAIRS - 1, 128)


def on_device(records, source_block, quality):
    vmem = pl.BlockSpec(memory_space=pltpu.VMEM)
    dma = pltpu.SemaphoreType.DMA
    sums = pl.pallas_call(
        kernel,
        out_shape=jax.ShapeDtypeStruct((COARSE, 128, 128), F32),
        in_specs=[pl.BlockSpec(memory_space=pl.ANY), pl.BlockSpec(memory_space=pltpu.SMEM), vmem],
        out_specs=vmem,
        scratch_shapes=[
            pltpu.VMEM((128, SHARE), F32),
            pltpu.VMEM((128, SHARE), F32),
            pltpu.VMEM((2, NY, 16, SHARE), BF16),
            pltpu.VMEM((NY, 16, SHARE), BF16),
            pltpu.VMEM((2, 2 * NZ, 16, PIECE), BF16),
            pltpu.VMEM((2, 16, PIECE), BF16),
            pltpu.VMEM((2, 2, 16, 2 * SHARE), BF16),
            pltpu.VMEM((2 * WIN, ROWS, 256), BF16),
            pltpu.VMEM((PAIRS, 128, 256), F32),
            pltpu.VMEM((PAIRS, 128, 256), BF16),
            pltpu.VMEM((2, 256, 2 * SHARE), BF16),
            pltpu.VMEM((2, 256, 128), BF16),
            pltpu.VMEM((PAIRS, 128, 256), F32),
            pltpu.VMEM((2, PAIRS, 128, 256), BF16),
            pltpu.VMEM((2, PAIRS, 128, 256), BF16),
            pltpu.VMEM((PAIRS, 128, 256), BF16),
            pltpu.VMEM((PAIRS, 128, 256), BF16),
            dma((NY,)), dma((NY,)), dma((2, 2 * NZ)), dma((2, 2 * NZ)), dma((2, 2 * NZ)), dma((2, 2 * NZ)),
            dma((WIN,)), dma((WIN,)), dma((2,)), dma((2,)),
            dma((2, PAIRS)), dma((2, PAIRS)), dma((PAIRS,)), dma((PAIRS,)),
            pltpu.SemaphoreType.REGULAR, dma((WIN,)),
        ],
        compiler_params=pltpu.CompilerParams(
            collective_id=0, has_side_effects=True, vmem_limit_bytes=56 << 20
        ),
        name="correlate",
    )(records, source_block, quality.reshape(1, 128))
    stacks = sums.reshape(COARSE, 2, FINE, 8, 128).transpose(1, 3, 0, 2, 4)
    return stacks.reshape(2, 8, COARSE * FINE, 128)[:, :, :LAGS]


def solution(mesh):
    in_specs = (P("rx", "tm"), P(), P("rx"))
    out_specs = P(None, "tm", None, "rx")
    return jax.shard_map(
        on_device, mesh=mesh, in_specs=in_specs, out_specs=out_specs, check_vma=False
    )
```
